32 devices in a mesh: group: 2 (over x), dom: 16 (over z, y, core).
Axes of the slice: x: 2, y: 2, z: 4, core: 2. Of those that a mesh axis runs over, the one named last changes fastest.
Arguments:
- fields: float32 [6, 35, 32768], P(None, None, ('group', 'dom')), may hold values from -6 to 6
- metric: float32 [9, 32768], P(None, ('group', 'dom')), may hold values from -3 to 3
- face_scale: float32 [4, 32768], P(None, ('group', 'dom')), may hold values from 0.5 to 10
- face_angles: float32 [2, 4, 32768], P(None, None, ('group', 'dom')), may hold values from -3.140625 to 3.140625
- neighbours: int32 [4, 32768], P(None, ('group', 'dom')), may hold values from -1 to 4479, as said below
- send_dom: int32 [2, 4096], P(None, ('group', 'dom')), may hold values from 0 to 4095, as said below
- send_partner: int32 [4096], P(('group', 'dom')), may hold values from 0 to 4095, as said below
- element_kind: int32 [32768], P(('group', 'dom')), may hold values from 0 to 6, as said below
- derivative: float32 [3, 35, 35], replicated, may hold values from -1 to 1
- lifting: float32 [35, 60], replicated, may hold values from -0.75 to 0.75
- block_inverse: bfloat16 [6, 210, 210], replicated
Outputs:
- advanced: float32 [6, 35, 32768], P(None, None, ('group', 'dom'))
The draws below stay inside these ranges and needn't reach their ends.
Inputs may be any that keep to these rules, and one draw needn't show every extreme that they name: `send_dom`: values are local face ids f * 1024 + e. Row 0 lists exactly the faces of the device whose neighbours slots are 4096 + i for i < 128, in the order of i; row 1 those with 4224 + i, in the order of i. `send_partner`: values are local face ids; exactly the faces of the device whose neighbours slot is 4352 + i, in the order of i. `neighbours`: on each device: every slot from 4096 up is read by exactly one face; 128 faces hold -1; every other face holds the id of another face of the same device, and that face holds its id. `element_kind`: elements of kind 1 or more (the fine region) lie exactly on the devices with group index 1 and dom index at least half of the dom axis; all elements of those devices have kind 1 or more, all others kind 0.
All inputs are finite; a program needn't handle non-finite values.
Results may differ from the reference program's by a relative error of at most 0.0003.
Values sent between devices are 32-bit elements; how exact they have to be, the bound alone decides.
A program may use at most 64 MiB of HBM per device.

```python
import jax
import jax.numpy as jnp
import numpy as np
from jax import lax

NC = 6
NP = 35
NFP = 15
KTYPES = 6
SWEEPS = 4
EL = 1024
NB = 128
NG = 128
NWALL = 128
TOTAL = 32768
N_GROUP = 2
N_DOM = 16


def face_plan(key):
    devices = N_GROUP * N_DOM
    face_total = 4 * EL

    def one_device(device_key):
        shuffled = jax.random.permutation(device_key, face_total).astype(jnp.int32)
        halo_faces = shuffled[:2 * NB]
        group_faces = shuffled[2 * NB:2 * NB + NG]
        wall_faces = shuffled[2 * NB + NG:2 * NB + NG + NWALL]
        paired = shuffled[2 * NB + NG + NWALL:].reshape(-1, 2)
        listed = jnp.zeros((face_total,), jnp.int32)
        listed = listed.at[halo_faces].set(face_total + jnp.arange(2 * NB, dtype=jnp.int32))
        listed = listed.at[group_faces].set(face_total + 2 * NB + jnp.arange(NG, dtype=jnp.int32))
        listed = listed.at[wall_faces].set(-1)
        listed = listed.at[paired[:, 0]].set(paired[:, 1])
        listed = listed.at[paired[:, 1]].set(paired[:, 0])
        return (listed, halo_faces.reshape(2, NB), group_faces)
    device_keys = jax.random.split(key, devices)
    return jax.vmap(one_device)(device_keys)


def draw_neighbours(key, part):
    listed = face_plan(jax.random.fold_in(key, 11))[0]
    devices = listed.shape[0]
    return jnp.transpose(listed.reshape(devices, 4, EL), (1, 0, 2)).reshape(4, devices * EL).astype(jnp.int32)


def draw_send_dom(key, part):
    halo_lists = face_plan(jax.random.fold_in(key, 11))[1]
    return jnp.transpose(halo_lists, (1, 0, 2)).reshape(2, -1).astype(jnp.int32)


def draw_send_partner(key, part):
    group_lists = face_plan(jax.random.fold_in(key, 11))[2]
    return group_lists.reshape(-1).astype(jnp.int32)


def draw_element_kind(key, part):
    devices = N_GROUP * N_DOM
    owner = jnp.arange(devices * EL, dtype=jnp.int32) // EL
    fine_region = (owner >= N_DOM) & (owner % N_DOM >= N_DOM // 2)
    shapes = jax.random.randint(key, (devices * EL,), 1, KTYPES + 1, dtype=jnp.int32)
    return jnp.where(fine_region, shapes, 0).astype(jnp.int32)


def draw_face_scale(key, part):
    devices = N_GROUP * N_DOM
    owner = jnp.arange(devices * EL, dtype=jnp.int32) // EL
    fine_region = (owner >= N_DOM) & (owner % N_DOM >= N_DOM // 2)
    low_end = jnp.where(fine_region, 2.5, 0.5).astype(jnp.float32)[None, :]
    unit = jax.random.uniform(jax.random.fold_in(key, 23), (4, devices * EL), jnp.float32, 0.0, 1.0)
    values = low_end * jnp.exp(unit * jnp.log(4.0))
    return jnp.clip(values, 0.5, 10.0).astype(jnp.float32)


def draw_block_inverse(key, part):
    order_n = NC * NP
    diag_key, off_key = jax.random.split(key)
    diagonal = jax.random.uniform(diag_key, (KTYPES, order_n), jnp.float32, 0.6, 1.0)
    spread = jax.random.normal(off_key, (KTYPES, order_n, order_n), jnp.float32) * 0.02
    identity = jnp.eye(order_n, dtype=jnp.float32)
    return (spread * (1.0 - identity) + identity * diagonal[:, :, None]).astype(jnp.bfloat16)


def block_scale(own_key, extent, shards, low, top_value):
    factor_of = 1.0
    for dim, blocks in shards:
        draws = jax.random.uniform(jax.random.fold_in(jax.random.fold_in(own_key, 6), dim), (blocks,), jnp.float32, low / len(shards), top_value / len(shards))
        factor_of = factor_of * jnp.repeat(jnp.exp(draws), extent[dim] // blocks).reshape((-1,) + (1,) * (len(extent) - 1 - dim))
    return factor_of


def bell_draw(own_key, dims, width, reach, shards=(), held_as=jnp.bfloat16):
    values = width * jax.random.normal(own_key, dims, jnp.float32)
    if shards:
        values = values * block_scale(own_key, dims, shards, -0.22, 0.18)
    return jnp.clip(values, -reach, reach).astype(held_as)


def setup_inputs(seed: int = 0) -> dict:
    keys = jax.random.split(jax.random.key(seed), 12)
    fields = bell_draw(keys[0], (NC, NP, TOTAL), 1.0, 6.0, ((2, 32),), jnp.float32)
    metric = bell_draw(keys[1], (9, TOTAL), 0.5, 3.0, ((1, 32),), jnp.float32)
    face_scale = draw_face_scale(jax.random.fold_in(keys[11], 71), 0)
    face_angles = jnp.clip(jax.random.uniform(keys[3], (2, 4, TOTAL), jnp.float32, -3.140625, 3.140625), -3.140625, 3.140625)
    neighbours = draw_neighbours(jax.random.fold_in(keys[11], 71), 0)
    send_dom = draw_send_dom(jax.random.fold_in(keys[11], 71), 0)
    send_partner = draw_send_partner(jax.random.fold_in(keys[11], 71), 0)
    element_kind = draw_element_kind(jax.random.fold_in(keys[11], 71), 0)
    derivative = bell_draw(keys[8], (3, NP, NP), NP ** -0.5, 1.0, (), jnp.float32)
    lifting = bell_draw(keys[9], (NP, 4 * NFP), (4 * NFP) ** -0.5, 0.75, (), jnp.float32)
    block_inverse = draw_block_inverse(jax.random.fold_in(keys[11], 71), 0)
    return {"fields": fields, "metric": metric, "face_scale": face_scale, "face_angles": face_angles, "neighbours": neighbours, "send_dom": send_dom, "send_partner": send_partner, "element_kind": element_kind, "derivative": derivative, "lifting": lifting, "block_inverse": block_inverse}


step_size = 0.2
highest = lax.Precision.HIGHEST


def face_nodes():
    lattice = []
    for along_r in range(5):
        for along_s in range(5 - along_r):
            for along_t in range(5 - along_r - along_s):
                lattice.append((along_r, along_s, along_t))
    checks = [lambda point: point[2] == 0, lambda point: point[1] == 0, lambda point: point[0] == 0, lambda point: point[0] + point[1] + point[2] == 4]
    chosen = []
    for check_of in checks:
        chosen.extend([position for position, point in enumerate(lattice) if check_of(point)])
    return np.array(chosen, dtype=np.int32)


def normals_of(face_angles):
    polar = face_angles[0]
    azimuth = face_angles[1]
    return jnp.stack([jnp.sin(polar) * jnp.cos(azimuth), jnp.sin(polar) * jnp.sin(azimuth), jnp.cos(polar)])


def trace_block(state_now):
    picked = state_now[:, face_nodes(), :]
    return picked.reshape(state_now.shape[0], 4, -1, state_now.shape[2])


def pool_of(traces):
    return jnp.transpose(traces, (0, 2, 1, 3)).reshape(traces.shape[0] * traces.shape[2], -1)


def exterior(trace_pool, neighbours, traces):
    flat_list = neighbours.reshape(-1)
    gathered = jnp.take(trace_pool, jnp.maximum(flat_list, 0), axis=1)
    gathered = gathered.reshape(traces.shape[0], traces.shape[2], traces.shape[1], traces.shape[3])
    gathered = jnp.transpose(gathered, (0, 2, 1, 3))
    mirror_sign = jnp.array([-1.0, -1.0, -1.0, 1.0, 1.0, 1.0], jnp.float32)
    mirrored = traces * mirror_sign[:, None, None, None]
    walled = (neighbours < 0)[None, :, None, :]
    return jnp.where(walled, mirrored, gathered)


def cross_product(left_vec, right_vec):
    return jnp.stack([left_vec[1] * right_vec[2] - left_vec[2] * right_vec[1],
                      left_vec[2] * right_vec[0] - left_vec[0] * right_vec[2],
                      left_vec[0] * right_vec[1] - left_vec[1] * right_vec[0]])


def surface(traces, normals, face_scale, lifting):
    electric = traces[:3]
    magnetic = traces[3:]
    normal_b = normals[:, :, None, :]
    along_e = jnp.sum(normal_b * electric, axis=0)
    along_h = jnp.sum(normal_b * magnetic, axis=0)
    flux_e = -cross_product(normal_b, magnetic) + along_e * normal_b - electric
    flux_h = cross_product(normal_b, electric) + along_h * normal_b - magnetic
    fluxes = jnp.concatenate([flux_e, flux_h]) * (0.5 * face_scale)[None, :, None, :]
    fluxes = fluxes.reshape(fluxes.shape[0], -1, fluxes.shape[3])
    return jnp.einsum("ij,cje->cie", lifting, fluxes, precision=highest, preferred_element_type=jnp.float32)


def volume(state_now, metric, derivative):
    grads = jnp.einsum("bij,cje->bcie", derivative, state_now, precision=highest, preferred_element_type=jnp.float32)

    def along(component, axis_no):
        return (metric[3 * axis_no] * grads[0, component] + metric[3 * axis_no + 1] * grads[1, component]
                + metric[3 * axis_no + 2] * grads[2, component])

    curl_h = jnp.stack([along(5, 1) - along(4, 2), along(3, 2) - along(5, 0), along(4, 0) - along(3, 1)])
    curl_e = jnp.stack([along(2, 1) - along(1, 2), along(0, 2) - along(2, 0), along(1, 0) - along(0, 1)])
    return jnp.concatenate([curl_h, -curl_e])


def apply_inverse(right_side, kinds, block_inverse):
    flattened = right_side.reshape(-1, right_side.shape[2])
    summed = jnp.zeros_like(flattened)
    for shape_no in range(block_inverse.shape[0]):
        matrix = block_inverse[shape_no].astype(jnp.float32)
        product = jnp.dot(matrix, flattened, precision=highest, preferred_element_type=jnp.float32)
        summed = summed + jnp.where(kinds == shape_no + 1, product, 0.0)
    return summed.reshape(right_side.shape)


def reference(fields, metric, face_scale, face_angles, neighbours, send_dom, send_partner, element_kind, derivative, lifting, block_inverse):
    devices = N_GROUP * N_DOM
    trace_rows = NC * NFP

    def blocks(array):
        leading = array.shape[:-1]
        return jnp.moveaxis(array.reshape(leading + (devices, EL)), -2, 0)

    field_b = blocks(fields)
    metric_b = blocks(metric)
    scale_b = blocks(face_scale)
    angle_b = blocks(face_angles)
    nbr_b = blocks(neighbours)
    kind_b = blocks(element_kind)
    dom_b = jnp.moveaxis(send_dom.reshape(2, devices, NB), 1, 0)
    part_b = send_partner.reshape(devices, NG)

    def outgoing(inputs):
        state_now, dom_list, part_list = inputs
        trace_pool = pool_of(trace_block(state_now))
        return jnp.take(trace_pool, dom_list.reshape(-1), axis=1), jnp.take(trace_pool, part_list, axis=1)

    def arrivals(current):
        dom_out, part_out = lax.map(outgoing, (current, dom_b, part_b))
        dom_out = dom_out.reshape(N_GROUP, N_DOM, trace_rows, 2 * NB)
        empty = jnp.zeros((N_GROUP, 1, trace_rows, NB), dom_out.dtype)
        from_prev = jnp.concatenate([empty, dom_out[:, :-1, :, NB:]], axis=1)
        from_next = jnp.concatenate([dom_out[:, 1:, :, :NB], empty], axis=1)
        partner = jnp.flip(part_out.reshape(N_GROUP, N_DOM, trace_rows, NG), axis=0)
        joined = jnp.concatenate([from_prev, from_next, partner], axis=3)
        return joined.reshape(devices, trace_rows, 2 * NB + NG)

    def explicit_step(inputs):
        state_now, arrived, metric_d, scale_d, angle_d, nbr_d = inputs
        normals = normals_of(angle_d)
        traces = trace_block(state_now)
        whole_pool = jnp.concatenate([pool_of(traces), arrived], axis=1)
        outside = exterior(whole_pool, nbr_d, traces)
        return state_now + step_size * (volume(state_now, metric_d, derivative) + surface(traces, normals, scale_d, lifting)
                                        - surface(outside, normals, scale_d, lifting))

    def sweep_step(inputs):
        state_now, current, arrived, scale_d, angle_d, nbr_d, kind_d = inputs
        normals = normals_of(angle_d)
        traces = trace_block(current)
        whole_pool = jnp.concatenate([pool_of(traces), arrived], axis=1)
        outside = exterior(whole_pool, nbr_d, traces)
        right_side = state_now - step_size * surface(outside, normals, scale_d, lifting)

        def solve_branch(operands):
            return apply_inverse(operands[0], operands[1], block_inverse)

        def empty_branch(operands):
            return jnp.zeros_like(operands[0])

        solved = lax.cond(jnp.any(kind_d > 0), solve_branch, empty_branch, (right_side, kind_d))
        return jnp.where(kind_d > 0, solved, state_now)

    arrived = arrivals(field_b)
    explicit = lax.map(explicit_step, (field_b, arrived, metric_b, scale_b, angle_b, nbr_b))
    current = field_b
    for sweep_no in range(SWEEPS):
        if sweep_no > 0:
            arrived = arrivals(current)
        current = lax.map(sweep_step, (field_b, current, arrived, scale_b, angle_b, nbr_b, kind_b))
    final = jnp.where(kind_b[:, None, None, :] > 0, current, explicit)
    return jnp.moveaxis(final, 0, -2).reshape(NC, NP, devices * EL)
```

```python
import functools

import jax
import jax.numpy as jnp
import numpy as np
from jax import lax
from jax.experimental import pallas as pl
from jax.experimental.pallas import tpu as pltpu
from jax.sharding import PartitionSpec as P

SWEEPS = 4
STEP = 0.2
NC, NP, NFP = 6, 35, 15
RP = 40
KP = 48
FP = 16
CHUNK = 512
SUB = 128
f32, bf16 = jnp.float32, jnp.bfloat16


def face_nodes():
    lattice = [(r, s, t) for r in range(5) for s in range(5 - r) for t in range(5 - r - s)]
    tests = [
        lambda p: p[2] == 0,
        lambda p: p[1] == 0,
        lambda p: p[0] == 0,
        lambda p: sum(p) == 4,
    ]
    return [[i for i, p in enumerate(lattice) if test(p)] for test in tests]


def constants():
    trace = np.zeros((4 * FP, NP), np.float32)
    for f, nodes in enumerate(face_nodes()):
        for n, node in enumerate(nodes):
            trace[f * FP + n, node] = 1
    trace3 = np.zeros((4 * FP, 3 * KP), np.float32)
    trace3[:, :NP] = trace
    trace3[:, 2 * KP : 2 * KP + NP] = trace
    spread = np.zeros((2, NP, 3 * KP), np.float32)
    for i in range(NP):
        spread[0, i, i] = spread[0, i, 2 * KP + i] = spread[1, i, KP + i] = 1
    lift_spread = np.zeros((2, 4 * NFP, 3 * 4 * FP), np.float32)
    for f in range(4):
        for n in range(NFP):
            row, col = f * NFP + n, f * FP + n
            lift_spread[0, row, col] = lift_spread[0, row, 8 * FP + col] = 1
            lift_spread[1, row, 4 * FP + col] = 1
    trace6 = np.kron(np.eye(NC, dtype=np.float32), trace)
    rows6 = np.kron(np.eye(NC, dtype=np.float32), np.eye(RP, NP, dtype=np.float32))
    cols6 = np.concatenate([rows6.T, rows6.T], axis=1)
    return [jnp.asarray(a, bf16) for a in (trace3, spread, lift_spread, trace6, rows6, cols6)]


def split(x):
    hi = x.astype(bf16)
    return hi, (x - hi.astype(f32)).astype(bf16)


def dot(a, b):
    return jnp.dot(a, b, preferred_element_type=f32)


def kernel(
    el, fields, metric, scale, angles, nb, send_dom, send_part, kind, deriv, lift, binv,
    trace3, spread, lift_spread, trace6, rows6, cols6,
    out,
    fpad, d3, l3, wt, wf, grads, tr, own, recv_n, coef, sel, sel_send, pool, remote, ext, rhs,
    sendbuf, recvbuf, send_sem, recv_sem,
):
    grp, dom = lax.axis_index("group"), lax.axis_index("dom")
    count = lax.axis_size("dom")
    half = count // 2
    fine = jnp.logical_and(grp == 1, dom >= half)
    halves = el // CHUNK
    chunks = 4 * halves
    has_prev, has_next = dom > 0, dom < count - 1
    fine_prev = jnp.logical_and(fine, dom > half)
    fine_next = jnp.logical_and(fine, has_next)

    barrier = pltpu.get_barrier_semaphore()

    @pl.when(has_prev)
    def _():
        pl.semaphore_signal(barrier, inc=1, device_id={"dom": dom - 1})

    @pl.when(has_next)
    def _():
        pl.semaphore_signal(barrier, inc=1, device_id={"dom": dom + 1})

    pl.semaphore_signal(barrier, inc=1, device_id={"group": 1 - grp})

    def slot(f):
        row = nb[f : f + 1, :]
        lane = lax.broadcasted_iota(jnp.int32, (1, el), 1)
        return jnp.where(row < 0, lane + f * el, row)

    def send_list():
        return jnp.concatenate([send_dom[0:1, :], send_dom[1:2, :], send_part[...]], axis=1)

    def pair_copies(step):
        targets = ({"dom": dom - 1}, {"dom": dom + 1}, {"group": 1 - grp})
        lands = (1, 0, 2)
        return [
            pltpu.make_async_remote_copy(
                src_ref=sendbuf.at[step, i],
                dst_ref=recvbuf.at[step, lands[i]],
                send_sem=send_sem.at[step, i],
                recv_sem=recv_sem.at[step, lands[i]],
                device_id=targets[i],
            )
            for i in range(3)
        ]

    def start(step, to_prev, to_next, partner):
        copies = pair_copies(step)

        @pl.when(to_prev)
        def _():
            copies[0].start()

        @pl.when(to_next)
        def _():
            copies[1].start()

        if partner:
            copies[2].start()

    def finish(step, from_prev, from_next, partner):
        copies = pair_copies(step)

        @pl.when(from_prev)
        def _():
            copies[0].wait_send()
            copies[1].wait_recv()
            remote[0] = recvbuf[step, 0]

        @pl.when(from_next)
        def _():
            copies[1].wait_send()
            copies[0].wait_recv()
            remote[1] = recvbuf[step, 1]

        if partner:
            copies[2].wait()
            remote[2] = recvbuf[step, 2]

    def pool_store(f, x):
        rows = x.shape[0]
        hi = x.astype(bf16).astype(f32)
        both = jnp.concatenate([hi, x - hi], axis=0).astype(bf16)
        for k in range(halves):
            h = f * halves + k
            pool[h * 2 * rows : (h + 1) * 2 * rows, :] = both[:, k * CHUNK : (k + 1) * CHUNK]

    def pick(y, which, rows):
        total = jnp.zeros((rows, y.shape[1]), f32)
        for h in range(chunks):
            at = h * 2 * rows
            value = y[at : at + rows] + y[at + rows : at + 2 * rows]
            total = jnp.where(which == h, value, total)
        return total

    def outgoing(step, rows):
        y = dot(pool[: chunks * 2 * rows, :], sel_send[...])
        picked = pick(y, send_list() // CHUNK, rows)
        for i in range(3):
            sendbuf[step, i, 0:rows, :] = picked[:, i * SUB : (i + 1) * SUB]

    def gather_local(rows, dest):
        for f in range(4):
            y = dot(pool[: chunks * 2 * rows, :], sel[:, f * el : (f + 1) * el])
            dest[f] = pick(y, slot(f) // CHUNK, rows)

    def gather_remote(rows, dest):
        x = jnp.concatenate([remote[i, 0:rows, :] for i in range(3)], axis=1)
        hi = x.astype(bf16).astype(f32)
        both = jnp.concatenate([hi, x - hi], axis=0).astype(bf16)
        for f in range(4):
            y = dot(both, sel[0 : 3 * SUB, f * el : (f + 1) * el])
            dest[f] = jnp.where(slot(f) // CHUNK == chunks, y[:rows] + y[rows:], dest[f])

    polar, azimuth = angles[0], angles[1]
    parts = (jnp.sin(polar), jnp.cos(polar), jnp.sin(azimuth), jnp.cos(azimuth))
    own[...] = jnp.zeros_like(own)
    for f in range(4):
        for i in range(4):
            own[f, i : i + 1, :] = parts[i][f : f + 1, :]
        w = 0.5 * scale[f : f + 1, :]
        sa, ca, sb, cb = (p[f : f + 1, :] for p in parts)
        for i, row in enumerate((w * ca * cb, w * ca * sb, -w * sa, -w * sb, w * cb)):
            coef[f, i : i + 1, :] = row
        pool_store(f, own[f])
        down = lax.broadcasted_iota(jnp.int32, (CHUNK, el), 0)
        sel[:, f * el : (f + 1) * el] = jnp.where(down == slot(f) % CHUNK, 1.0, 0.0).astype(bf16)
    down = lax.broadcasted_iota(jnp.int32, (CHUNK, 3 * SUB), 0)
    sel_send[...] = jnp.where(down == send_list() % CHUNK, 1.0, 0.0).astype(bf16)
    remote[...] = jnp.zeros_like(remote)
    sendbuf[0] = jnp.zeros_like(sendbuf[0])

    outgoing(0, 8)
    pl.semaphore_wait(
        barrier, 1 + has_prev.astype(jnp.int32) + has_next.astype(jnp.int32)
    )
    start(0, has_prev, has_next, True)

    gather_local(8, recv_n)

    fpad[...] = jnp.zeros_like(fpad)
    d3[...] = jnp.zeros_like(d3)
    l3[...] = jnp.zeros_like(l3)
    for b in range(3):
        hi, lo = split(deriv[b])
        d3[b * RP : b * RP + NP, :] = dot(hi, spread[0]) + dot(lo, spread[1])
    d3[3 * RP : 3 * RP + 4 * FP, :] = trace3[...].astype(f32)
    hi, lo = split(lift[...])
    l3[0:NP, :] = dot(hi, lift_spread[0]) + dot(lo, lift_spread[1])
    d3b = d3[...].astype(bf16)
    for c in range(NC):
        fpad[c, 0:NP, :] = fields[c]
        hi, lo = split(fpad[c])
        y = dot(d3b, jnp.concatenate([hi, hi, lo], axis=0))
        grads[c] = y[: 3 * RP]
        tr[c * 4 * FP : (c + 1) * 4 * FP, :] = y[3 * RP :]

    def trace_pq(f, n_ref, sign):
        at = [tr[c * 4 * FP + f * FP : c * 4 * FP + (f + 1) * FP, :] for c in range(NC)]
        sa, ca, sb, cb = (n_ref[f, i : i + 1, :] for i in range(4))
        if sign is not None:
            at[:3] = [sign * e for e in at[:3]]
        e_t = ca * (cb * at[0] + sb * at[1]) - sa * at[2]
        e_p = cb * at[1] - sb * at[0]
        h_t = ca * (cb * at[3] + sb * at[4]) - sa * at[5]
        h_p = cb * at[4] - sb * at[3]
        return jnp.concatenate([h_p - e_t, -h_t - e_p], axis=0)

    def fill_pool():
        for f in range(4):
            sign = jnp.where(nb[f : f + 1, :] < 0, -1.0, 1.0)
            pool_store(f, trace_pq(f, recv_n, sign))

    def lifted(pq):
        for c in range(NC):
            rows = []
            for f in range(4):
                p, q = pq[f][:FP], pq[f][FP:]
                a, b = (p, q) if c < 3 else (q, -p)
                k = c % 3
                row = coef[f, k : k + 1, :] * a
                if k < 2:
                    row = row + coef[f, 3 + k : 4 + k, :] * b
                rows.append(row)
            hi, lo = split(jnp.concatenate(rows, axis=0))
            yield c, dot(l3[...].astype(bf16), jnp.concatenate([hi, hi, lo], axis=0))

    finish(0, has_prev, has_next, True)
    gather_remote(8, recv_n)
    fill_pool()
    outgoing(1, 2 * FP)
    start(1, has_prev, has_next, True)
    gather_local(2 * FP, ext)

    @pl.when(fine)
    def _():
        for k in range(binv.shape[0]):
            b2 = dot(binv[k], cols6[...]).astype(bf16)
            wt[k] = dot(trace6[...], b2).astype(bf16)
            wf[k] = dot(rows6[...], b2).astype(bf16)

    remote[...] = jnp.zeros_like(remote)
    finish(1, has_prev, has_next, True)
    gather_remote(2 * FP, ext)

    @pl.when(jnp.logical_not(fine))
    def _():
        pq = [trace_pq(f, own, None) - ext[f] for f in range(4)]

        def along(c, axis):
            return sum(
                metric[3 * axis + b : 3 * axis + b + 1, :] * grads[c, b * RP : (b + 1) * RP, :]
                for b in range(3)
            )

        for c, s in lifted(pq):
            k, other = c % 3, 3 - 3 * (c // 3)
            one, two = (k + 1) % 3, (k + 2) % 3
            curl = along(other + two, one) - along(other + one, two)
            vol = curl if c < 3 else -curl
            out[c] = (fpad[c, 0:RP, :] + STEP * (vol + s))[:NP]

    @pl.when(fine)
    def _():
        def right_side():
            terms = [
                fpad[c, 0:RP, :] - STEP * s for c, s in lifted([ext[f] for f in range(4)])
            ]
            hi, lo = split(jnp.concatenate(terms, axis=0))
            rhs[0 : NC * RP, :] = hi
            rhs[NC * RP : 2 * NC * RP, :] = lo

        def blocks(weights, k):
            mask = jnp.where(kind[...] == k + 1, 1.0, 0.0).astype(bf16)
            return dot(weights[k], rhs[...] * mask)

        def sweep(no, carry):
            right_side()
            tr[...] = blocks(wt, 0)
            for k in range(1, binv.shape[0]):
                tr[...] += blocks(wt, k)
            fill_pool()
            outgoing(no, 2 * FP)
            start(no, fine_prev, fine_next, False)
            gather_local(2 * FP, ext)
            finish(no, fine_prev, fine_next, False)
            gather_remote(2 * FP, ext)
            return carry

        lax.fori_loop(2, SWEEPS + 1, sweep, 0)
        right_side()
        total = blocks(wf, 0)
        for k in range(1, binv.shape[0]):
            total += blocks(wf, k)
        for c in range(NC):
            out[c] = total[c * RP : c * RP + NP]


def shards(*args):
    (fields, metric, scale, angles, nb, send_dom, send_part, kind, deriv, lift, binv) = args
    el = fields.shape[2]
    kinds = binv.shape[0]
    operands = [
        fields, metric, scale, angles, nb, send_dom, send_part.reshape(1, -1),
        kind.reshape(1, -1), deriv, lift, binv, *constants(),
    ]
    vmem = pltpu.VMEM
    return pl.pallas_call(
        functools.partial(kernel, el),
        out_shape=jax.ShapeDtypeStruct(fields.shape, f32),
        in_specs=[pl.BlockSpec(memory_space=vmem)] * len(operands),
        out_specs=pl.BlockSpec(memory_space=vmem),
        scratch_shapes=[
            vmem((NC, KP, el), f32),
            vmem((3 * RP + 4 * FP, 3 * KP), f32),
            vmem((RP, 12 * FP), f32),
            vmem((kinds, NC * 4 * FP, 2 * NC * RP), bf16),
            vmem((kinds, NC * RP, 2 * NC * RP), bf16),
            vmem((NC, 3 * RP, el), f32),
            vmem((NC * 4 * FP, el), f32),
            vmem((4, 8, el), f32),
            vmem((4, 8, el), f32),
            vmem((4, 8, el), f32),
            vmem((CHUNK, 4 * el), bf16),
            vmem((CHUNK, 3 * SUB), bf16),
            vmem((4 * (el // CHUNK) * 4 * FP, CHUNK), bf16),
            vmem((3, 2 * FP, SUB), f32),
            vmem((4, 2 * FP, el), f32),
            vmem((2 * NC * RP, el), bf16),
            vmem((SWEEPS + 1, 3, 2 * FP, SUB), f32),
            vmem((SWEEPS + 1, 3, 2 * FP, SUB), f32),
            pltpu.SemaphoreType.DMA((SWEEPS + 1, 3)),
            pltpu.SemaphoreType.DMA((SWEEPS + 1, 3)),
        ],
        compiler_params=pltpu.CompilerParams(
            collective_id=0, has_side_effects=True, vmem_limit_bytes=56 * 2**20
        ),
    )(*operands)


def solution(mesh):
    both = ("group", "dom")
    in_specs = (
        P(None, None, both), P(None, both), P(None, both), P(None, None, both), P(None, both),
        P(None, both), P(both), P(both), P(), P(), P(),
    )
    return jax.shard_map(
        shards, mesh=mesh, in_specs=in_specs, out_specs=P(None, None, both), check_vma=False
    )
```

```python
import functools

import jax
import jax.numpy as jnp
import numpy as np
from jax import lax
from jax.experimental import pallas as pl
from jax.experimental.pallas import tpu as pltpu
from jax.sharding import PartitionSpec as P

SWEEPS = 4
STEP = 0.2
NC, NP, NFP = 6, 35, 15
RP = 40
KP = 48
FP = 16
BK = 512
CHUNK = 512
SUB = 128
f32, bf16 = jnp.float32, jnp.bfloat16


def face_nodes():
    lattice = [(r, s, t) for r in range(5) for s in range(5 - r) for t in range(5 - r - s)]
    tests = [
        lambda p: p[2] == 0,
        lambda p: p[1] == 0,
        lambda p: p[0] == 0,
        lambda p: sum(p) == 4,
    ]
    return [[i for i, p in enumerate(lattice) if test(p)] for test in tests]


def constants():
    trace = np.zeros((4 * FP, NP), np.float32)
    for f, nodes in enumerate(face_nodes()):
        for n, node in enumerate(nodes):
            trace[f * FP + n, node] = 1
    trace3 = np.zeros((4 * FP, 3 * KP), np.float32)
    trace3[:, :NP] = trace
    trace3[:, 2 * KP : 2 * KP + NP] = trace
    spread = np.zeros((2, NP, 3 * KP), np.float32)
    for i in range(NP):
        spread[0, i, i] = spread[0, i, 2 * KP + i] = spread[1, i, KP + i] = 1
    lift_spread = np.zeros((2, 4 * NFP, 3 * 4 * FP), np.float32)
    for f in range(4):
        for n in range(NFP):
            row, col = f * NFP + n, f * FP + n
            lift_spread[0, row, col] = lift_spread[0, row, 8 * FP + col] = 1
            lift_spread[1, row, 4 * FP + col] = 1
    trace6 = np.kron(np.eye(NC, dtype=np.float32), trace)
    rows6 = np.kron(np.eye(NC, dtype=np.float32), np.eye(RP, NP, dtype=np.float32))
    cols6 = np.zeros((NC * NP, BK), np.float32)
    cols6[:, : 2 * NC * RP] = np.concatenate([rows6.T, rows6.T], axis=1)
    return [jnp.asarray(a, bf16) for a in (trace3, spread, lift_spread, trace6, rows6, cols6)]


def split(x):
    hi = x.astype(bf16)
    return hi, (x - hi.astype(f32)).astype(bf16)


def dot(a, b):
    return jnp.dot(a, b, preferred_element_type=f32)


def kernel(
    el, fields, metric, scale, angles, nb, send_dom, send_part, kind, deriv, lift, binv,
    trace3, spread, lift_spread, trace6, rows6, cols6,
    out,
    fpad, d3, l3, wt, wf, grads, tr, own, recv_n, coef, sel, sel_send, pool, remote, ext,
    base, lb, rhs6, sendbuf, recvbuf, send_sem, recv_sem,
):
    grp, dom = lax.axis_index("group"), lax.axis_index("dom")
    count = lax.axis_size("dom")
    half = count // 2
    fine = jnp.logical_and(grp == 1, dom >= half)
    halves = el // CHUNK
    chunks = 4 * halves
    has_prev, has_next = dom > 0, dom < count - 1
    fine_prev = jnp.logical_and(fine, dom > half)
    fine_next = jnp.logical_and(fine, has_next)

    barrier = pltpu.get_barrier_semaphore()

    @pl.when(has_prev)
    def _():
        pl.semaphore_signal(barrier, inc=1, device_id={"dom": dom - 1})

    @pl.when(has_next)
    def _():
        pl.semaphore_signal(barrier, inc=1, device_id={"dom": dom + 1})

    pl.semaphore_signal(barrier, inc=1, device_id={"group": 1 - grp})

    def slot(f):
        row = nb[f : f + 1, :]
        lane = lax.broadcasted_iota(jnp.int32, (1, el), 1)
        return jnp.where(row < 0, lane + f * el, row)

    def send_list():
        return jnp.concatenate([send_dom[0:1, :], send_dom[1:2, :], send_part[...]], axis=1)

    def pair_copies(step):
        targets = ({"dom": dom - 1}, {"dom": dom + 1}, {"group": 1 - grp})
        lands = (1, 0, 2)
        return [
            pltpu.make_async_remote_copy(
                src_ref=sendbuf.at[step, i],
                dst_ref=recvbuf.at[step, lands[i]],
                send_sem=send_sem.at[step, i],
                recv_sem=recv_sem.at[step, lands[i]],
                device_id=targets[i],
            )
            for i in range(3)
        ]

    def start(step, to_prev, to_next, partner):
        copies = pair_copies(step)

        @pl.when(to_prev)
        def _():
            copies[0].start()

        @pl.when(to_next)
        def _():
            copies[1].start()

        if partner:
            copies[2].start()

    def finish(step, from_prev, from_next, partner):
        copies = pair_copies(step)

        @pl.when(from_prev)
        def _():
            copies[0].wait_send()
            copies[1].wait_recv()
            remote[0] = recvbuf[step, 0]

        @pl.when(from_next)
        def _():
            copies[1].wait_send()
            copies[0].wait_recv()
            remote[1] = recvbuf[step, 1]

        if partner:
            copies[2].wait()
            remote[2] = recvbuf[step, 2]

    def pool_store(f, x):
        rows = x.shape[0]
        hi = x.astype(bf16).astype(f32)
        both = jnp.concatenate([hi, x - hi], axis=0).astype(bf16)
        for k in range(halves):
            h = f * halves + k
            pool[h * 2 * rows : (h + 1) * 2 * rows, :] = both[:, k * CHUNK : (k + 1) * CHUNK]

    def pick(y, which, rows, count, total=None):
        if total is None:
            total = jnp.zeros((rows, y.shape[1]), f32)
        for h in range(count):
            at = h * 2 * rows
            value = y[at : at + rows] + y[at + rows : at + 2 * rows]
            total = jnp.where(which == h, value, total)
        return total

    def outgoing(step, rows, lists):
        cols = lists * SUB
        y = dot(pool[: chunks * 2 * rows, :], sel_send[:, :cols])
        picked = pick(y, (send_list() // CHUNK)[:, :cols], rows, chunks)
        for i in range(lists):
            sendbuf[step, i, 0:rows, :] = picked[:, i * SUB : (i + 1) * SUB]

    def arrived(rows, lists):
        x = jnp.concatenate([remote[i, 0:rows, :] for i in range(lists)], axis=1)
        hi = x.astype(bf16).astype(f32)
        return jnp.concatenate([hi, x - hi], axis=0).astype(bf16)

    def gather_all(rows, dest):
        at = chunks * 2 * rows
        pool[at : at + 2 * rows, :] = jnp.zeros((2 * rows, CHUNK), bf16)
        pool[at : at + 2 * rows, 0 : 3 * SUB] = arrived(rows, 3)
        for f in range(4):
            y = dot(pool[: at + 2 * rows, :], sel[:, f * el : (f + 1) * el])
            dest[f] = pick(y, slot(f) // CHUNK, rows, chunks + 1)

    def gather_local(rows, dest):
        for f in range(4):
            y = dot(pool[: chunks * 2 * rows, :], sel[:, f * el : (f + 1) * el])
            dest[f] = pick(y, slot(f) // CHUNK, rows, chunks, base[f])

    def gather_dom(rows, dest):
        both = arrived(rows, 2)
        for f in range(4):
            y = dot(both, sel[0 : 2 * SUB, f * el : (f + 1) * el])
            there = slot(f) // (2 * SUB) == 4 * el // (2 * SUB)
            dest[f] = jnp.where(there, y[:rows] + y[rows:], dest[f])

    polar, azimuth = angles[0], angles[1]
    parts = (jnp.sin(polar), jnp.cos(polar), jnp.sin(azimuth), jnp.cos(azimuth))
    own[...] = jnp.zeros_like(own)
    for f in range(4):
        for i in range(4):
            own[f, i : i + 1, :] = parts[i][f : f + 1, :]
        w = 0.5 * scale[f : f + 1, :]
        sa, ca, sb, cb = (p[f : f + 1, :] for p in parts)
        for i, row in enumerate((w * ca * cb, w * ca * sb, -w * sa, -w * sb, w * cb)):
            coef[f, i : i + 1, :] = row
        pool_store(f, own[f])
    down = lax.broadcasted_iota(jnp.int32, (CHUNK, 3 * SUB), 0)
    sel_send[...] = jnp.where(down == send_list() % CHUNK, 1.0, 0.0).astype(bf16)
    remote[...] = jnp.zeros_like(remote)
    sendbuf[0] = jnp.zeros_like(sendbuf[0])

    outgoing(0, 8, 3)
    pl.semaphore_wait(
        barrier, 1 + has_prev.astype(jnp.int32) + has_next.astype(jnp.int32)
    )
    start(0, has_prev, has_next, True)

    for f in range(4):
        down = lax.broadcasted_iota(jnp.int32, (CHUNK, el), 0)
        sel[:, f * el : (f + 1) * el] = jnp.where(down == slot(f) % CHUNK, 1.0, 0.0).astype(bf16)

    fpad[...] = jnp.zeros_like(fpad)
    d3[...] = jnp.zeros_like(d3)
    l3[...] = jnp.zeros_like(l3)
    for b in range(3):
        hi, lo = split(deriv[b])
        d3[b * RP : b * RP + NP, :] = dot(hi, spread[0]) + dot(lo, spread[1])
    d3[3 * RP : 3 * RP + 4 * FP, :] = trace3[...].astype(f32)
    hi, lo = split(lift[...])
    l3[0:NP, :] = dot(hi, lift_spread[0]) + dot(lo, lift_spread[1])
    lane = lax.broadcasted_iota(jnp.int32, l3.shape, 1)
    lb[...] = jnp.concatenate(
        [jnp.where(lane // FP % 4 == f, l3[...], 0.0) for f in range(4)], axis=0
    ).astype(bf16)
    d3b = d3[...].astype(bf16)
    for c in range(NC):
        fpad[c, 0:NP, :] = fields[c]
        hi, lo = split(fpad[c])
        y = dot(d3b, jnp.concatenate([hi, hi, lo], axis=0))
        grads[c] = y[: 3 * RP]
        tr[c * 4 * FP : (c + 1) * 4 * FP, :] = y[3 * RP :]

    def trace_pq(f, n_ref, sign):
        at = [tr[c * 4 * FP + f * FP : c * 4 * FP + (f + 1) * FP, :] for c in range(NC)]
        sa, ca, sb, cb = (n_ref[f, i : i + 1, :] for i in range(4))
        if sign is not None:
            at[:3] = [sign * e for e in at[:3]]
        e_t = ca * (cb * at[0] + sb * at[1]) - sa * at[2]
        e_p = cb * at[1] - sb * at[0]
        h_t = ca * (cb * at[3] + sb * at[4]) - sa * at[5]
        h_p = cb * at[4] - sb * at[3]
        return jnp.concatenate([h_p - e_t, -h_t - e_p], axis=0)

    def fill_pool():
        for f in range(4):
            sign = jnp.where(nb[f : f + 1, :] < 0, -1.0, 1.0)
            pool_store(f, trace_pq(f, recv_n, sign))

    def lifted(pq):
        halves_of = []
        for at in (0, FP):
            hi, lo = split(jnp.concatenate([pq[f][at : at + FP] for f in range(4)], axis=0))
            halves_of.append(dot(lb[...], jnp.concatenate([hi, hi, lo], axis=0)))
        lp, lq = halves_of
        for c in range(NC):
            k, total = c % 3, 0.0
            a, b = (lp, lq) if c < 3 else (lq, lp)
            for f in range(4):
                at = slice(f * RP, (f + 1) * RP)
                total = total + coef[f, k : k + 1, :] * a[at]
                if k < 2:
                    term = coef[f, 3 + k : 4 + k, :] * b[at]
                    total = total + term if c < 3 else total - term
            yield c, total

    finish(0, has_prev, has_next, True)
    gather_all(8, recv_n)
    fill_pool()
    outgoing(1, 2 * FP, 3)
    start(1, has_prev, has_next, True)

    @pl.when(fine)
    def _():
        rhs6[...] = jnp.zeros_like(rhs6)
        for k in range(binv.shape[0]):
            b2 = dot(binv[k], cols6[...]).astype(bf16)
            wt[:, k * BK : (k + 1) * BK] = dot(trace6[...], b2).astype(bf16)
            wf[:, k * BK : (k + 1) * BK] = dot(rows6[...], b2).astype(bf16)

    remote[...] = jnp.zeros_like(remote)
    finish(1, has_prev, has_next, True)
    gather_all(2 * FP, ext)

    @pl.when(jnp.logical_not(fine))
    def _():
        pq = [trace_pq(f, own, None) - ext[f] for f in range(4)]

        def along(c, axis):
            return sum(
                metric[3 * axis + b : 3 * axis + b + 1, :] * grads[c, b * RP : (b + 1) * RP, :]
                for b in range(3)
            )

        for c, s in lifted(pq):
            k, other = c % 3, 3 - 3 * (c // 3)
            one, two = (k + 1) % 3, (k + 2) % 3
            curl = along(other + two, one) - along(other + one, two)
            vol = curl if c < 3 else -curl
            out[c] = (fpad[c, 0:RP, :] + STEP * (vol + s))[:NP]

    @pl.when(fine)
    def _():
        def right_side():
            terms = [
                fpad[c, 0:RP, :] - STEP * s for c, s in lifted([ext[f] for f in range(4)])
            ]
            both = jnp.concatenate(split(jnp.concatenate(terms, axis=0)), axis=0)
            for k in range(binv.shape[0]):
                mask = jnp.where(kind[...] == k + 1, 1.0, 0.0).astype(bf16)
                rhs6[k * BK : k * BK + 2 * NC * RP, :] = both * mask

        for f in range(4):
            base[f] = jnp.where(slot(f) >= 4 * el + 2 * SUB, ext[f], 0.0)

        def sweep(no, carry):
            right_side()
            tr[...] = dot(wt[...], rhs6[...])
            fill_pool()
            outgoing(no, 2 * FP, 2)
            start(no, fine_prev, fine_next, False)
            gather_local(2 * FP, ext)
            finish(no, fine_prev, fine_next, False)
            gather_dom(2 * FP, ext)
            return carry

        lax.fori_loop(2, SWEEPS + 1, sweep, 0)
        right_side()
        total = dot(wf[...], rhs6[...])
        for c in range(NC):
            out[c] = total[c * RP : c * RP + NP]


def shards(*args):
    (fields, metric, scale, angles, nb, send_dom, send_part, kind, deriv, lift, binv) = args
    el = fields.shape[2]
    kinds = binv.shape[0]
    operands = [
        fields, metric, scale, angles, nb, send_dom, send_part.reshape(1, -1),
        kind.reshape(1, -1), deriv, lift, binv, *constants(),
    ]
    vmem = pltpu.VMEM
    return pl.pallas_call(
        functools.partial(kernel, el),
        out_shape=jax.ShapeDtypeStruct(fields.shape, f32),
        in_specs=[pl.BlockSpec(memory_space=vmem)] * len(operands),
        out_specs=pl.BlockSpec(memory_space=vmem),
        scratch_shapes=[
            vmem((NC, KP, el), f32),
            vmem((3 * RP + 4 * FP, 3 * KP), f32),
            vmem((RP, 12 * FP), f32),
            vmem((NC * 4 * FP, kinds * BK), bf16),
            vmem((NC * RP, kinds * BK), bf16),
            vmem((NC, 3 * RP, el), f32),
            vmem((NC * 4 * FP, el), f32),
            vmem((4, 8, el), f32),
            vmem((4, 8, el), f32),
            vmem((4, 8, el), f32),
            vmem((CHUNK, 4 * el), bf16),
            vmem((CHUNK, 3 * SUB), bf16),
            vmem(((4 * (el // CHUNK) + 1) * 4 * FP, CHUNK), bf16),
            vmem((3, 2 * FP, SUB), f32),
            vmem((4, 2 * FP, el), f32),
            vmem((4, 2 * FP, el), f32),
            vmem((4 * RP, 12 * FP), bf16),
            vmem((kinds * BK, el), bf16),
            vmem((SWEEPS + 1, 3, 2 * FP, SUB), f32),
            vmem((SWEEPS + 1, 3, 2 * FP, SUB), f32),
            pltpu.SemaphoreType.DMA((SWEEPS + 1, 3)),
            pltpu.SemaphoreType.DMA((SWEEPS + 1, 3)),
        ],
        compiler_params=pltpu.CompilerParams(
            collective_id=0, has_side_effects=True, vmem_limit_bytes=56 * 2**20
        ),
    )(*operands)


def solution(mesh):
    both = ("group", "dom")
    in_specs = (
        P(None, None, both), P(None, both), P(None, both), P(None, None, both), P(None, both),
        P(None, both), P(both), P(both), P(), P(), P(),
    )
    return jax.shard_map(
        shards, mesh=mesh, in_specs=in_specs, out_specs=P(None, None, both), check_vma=False
    )
```

```python
import functools

import jax
import jax.numpy as jnp
import numpy as np
from jax import lax
from jax.experimental import pallas as pl
from jax.experimental.pallas import tpu as pltpu
from jax.sharding import PartitionSpec as P

SWEEPS = 4
STEP = 0.2
NC, NP, NFP = 6, 35, 15
RP = 40
KP = 48
FP = 16
BK = 512
CHUNK = 512
SUB = 128
f32, bf16 = jnp.float32, jnp.bfloat16


def face_nodes():
    lattice = [(r, s, t) for r in range(5) for s in range(5 - r) for t in range(5 - r - s)]
    tests = [
        lambda p: p[2] == 0,
        lambda p: p[1] == 0,
        lambda p: p[0] == 0,
        lambda p: sum(p) == 4,
    ]
    return [[i for i, p in enumerate(lattice) if test(p)] for test in tests]


def constants():
    trace = np.zeros((4 * FP, NP), np.float32)
    for f, nodes in enumerate(face_nodes()):
        for n, node in enumerate(nodes):
            trace[f * FP + n, node] = 1
    trace3 = np.zeros((4 * FP, 3 * KP), np.float32)
    trace3[:, :NP] = trace
    trace3[:, 2 * KP : 2 * KP + NP] = trace
    spread = np.zeros((2, NP, 3 * KP), np.float32)
    for i in range(NP):
        spread[0, i, i] = spread[0, i, 2 * KP + i] = spread[1, i, KP + i] = 1
    lift_spread = np.zeros((2, 4 * NFP, 3 * 4 * FP), np.float32)
    for f in range(4):
        for n in range(NFP):
            row, col = f * NFP + n, f * FP + n
            lift_spread[0, row, col] = lift_spread[0, row, 8 * FP + col] = 1
            lift_spread[1, row, 4 * FP + col] = 1
    trace6 = np.kron(np.eye(NC, dtype=np.float32), trace)
    rows6 = np.kron(np.eye(NC, dtype=np.float32), np.eye(RP, NP, dtype=np.float32))
    cols6 = np.zeros((NC * NP, BK // 2), np.float32)
    cols6[:, : NC * RP] = rows6.T
    return [jnp.asarray(a, bf16) for a in (trace3, spread, lift_spread, trace6, rows6, cols6)]


def split(x):
    hi = x.astype(bf16)
    return hi, (x - hi.astype(f32)).astype(bf16)


def dot(a, b):
    return jnp.dot(a, b, preferred_element_type=f32)


def kernel(
    el, fields, metric, scale, angles, nb, send_dom, send_part, kind, deriv, lift, binv,
    trace3, spread, lift_spread, trace6, rows6, cols6,
    out,
    fpad, d3, l3, wt, wf, grads, tr, own, recv_n, coef, sel, sel_send, pool, remote, ext,
    base, lb, rhs6, sendbuf, recvbuf, send_sem, recv_sem,
):
    grp, dom = lax.axis_index("group"), lax.axis_index("dom")
    count = lax.axis_size("dom")
    half = count // 2
    fine = jnp.logical_and(grp == 1, dom >= half)
    halves = el // CHUNK
    chunks = 4 * halves
    has_prev, has_next = dom > 0, dom < count - 1
    fine_prev = jnp.logical_and(fine, dom > half)
    fine_next = jnp.logical_and(fine, has_next)

    barrier = pltpu.get_barrier_semaphore()

    @pl.when(has_prev)
    def _():
        pl.semaphore_signal(barrier, inc=1, device_id={"dom": dom - 1})

    @pl.when(has_next)
    def _():
        pl.semaphore_signal(barrier, inc=1, device_id={"dom": dom + 1})

    pl.semaphore_signal(barrier, inc=1, device_id={"group": 1 - grp})

    def slot(f):
        row = nb[f : f + 1, :]
        lane = lax.broadcasted_iota(jnp.int32, (1, el), 1)
        return jnp.where(row < 0, lane + f * el, row)

    def send_list():
        return jnp.concatenate([send_dom[0:1, :], send_dom[1:2, :], send_part[...]], axis=1)

    def pair_copies(step):
        targets = ({"dom": dom - 1}, {"dom": dom + 1}, {"group": 1 - grp})
        lands = (1, 0, 2)
        return [
            pltpu.make_async_remote_copy(
                src_ref=sendbuf.at[step, i],
                dst_ref=recvbuf.at[step, lands[i]],
                send_sem=send_sem.at[step, i],
                recv_sem=recv_sem.at[step, lands[i]],
                device_id=targets[i],
            )
            for i in range(3)
        ]

    def start(step, to_prev, to_next, partner):
        copies = pair_copies(step)

        @pl.when(to_prev)
        def _():
            copies[0].start()

        @pl.when(to_next)
        def _():
            copies[1].start()

        if partner:
            copies[2].start()

    def finish(step, from_prev, from_next, partner):
        copies = pair_copies(step)

        @pl.when(from_prev)
        def _():
            copies[0].wait_send()
            copies[1].wait_recv()
            remote[0] = recvbuf[step, 0]

        @pl.when(from_next)
        def _():
            copies[1].wait_send()
            copies[0].wait_recv()
            remote[1] = recvbuf[step, 1]

        if partner:
            copies[2].wait()
            remote[2] = recvbuf[step, 2]

    def pool_store(f, x):
        rows = x.shape[0]
        hi = x.astype(bf16).astype(f32)
        both = jnp.concatenate([hi, x - hi], axis=0).astype(bf16)
        for k in range(halves):
            h = f * halves + k
            pool[h * 2 * rows : (h + 1) * 2 * rows, :] = both[:, k * CHUNK : (k + 1) * CHUNK]

    def pick(y, which, rows, count, total=None):
        if total is None:
            total = jnp.zeros((rows, y.shape[1]), f32)
        for h in range(count):
            at = h * 2 * rows
            value = y[at : at + rows] + y[at + rows : at + 2 * rows]
            total = jnp.where(which == h, value, total)
        return total

    def outgoing(step, rows, lists):
        cols = lists * SUB
        y = dot(pool[: chunks * 2 * rows, :], sel_send[:, :cols])
        picked = pick(y, (send_list() // CHUNK)[:, :cols], rows, chunks)
        for i in range(lists):
            sendbuf[step, i, 0:rows, :] = picked[:, i * SUB : (i + 1) * SUB]

    def arrived(rows, lists):
        x = jnp.concatenate([remote[i, 0:rows, :] for i in range(lists)], axis=1)
        hi = x.astype(bf16).astype(f32)
        return jnp.concatenate([hi, x - hi], axis=0).astype(bf16)

    def gather_all(rows, dest):
        at = chunks * 2 * rows
        pool[at : at + 2 * rows, :] = jnp.zeros((2 * rows, CHUNK), bf16)
        pool[at : at + 2 * rows, 0 : 3 * SUB] = arrived(rows, 3)
        for f in range(4):
            y = dot(pool[: at + 2 * rows, :], sel[:, f * el : (f + 1) * el])
            dest[f] = pick(y, slot(f) // CHUNK, rows, chunks + 1)

    def gather_local(rows, dest, start_from=None):
        for f in range(4):
            y = dot(pool[: chunks * 2 * rows, :], sel[:, f * el : (f + 1) * el])
            dest[f] = pick(
                y, slot(f) // CHUNK, rows, chunks, None if start_from is None else start_from[f]
            )

    def gather_late(rows, dest, lists):
        both = arrived(rows, lists)
        for f in range(4):
            y = dot(both, sel[0 : lists * SUB, f * el : (f + 1) * el])
            here = slot(f)
            there = jnp.logical_and(here >= 4 * el, here < 4 * el + lists * SUB)
            dest[f] = jnp.where(there, y[:rows] + y[rows:], dest[f])

    polar, azimuth = angles[0], angles[1]
    parts = (jnp.sin(polar), jnp.cos(polar), jnp.sin(azimuth), jnp.cos(azimuth))
    own[...] = jnp.zeros_like(own)
    for f in range(4):
        for i in range(4):
            own[f, i : i + 1, :] = parts[i][f : f + 1, :]
        w = 0.5 * scale[f : f + 1, :]
        sa, ca, sb, cb = (p[f : f + 1, :] for p in parts)
        for i, row in enumerate((w * ca * cb, w * ca * sb, -w * sa, -w * sb, w * cb)):
            coef[f, i : i + 1, :] = row
        pool_store(f, own[f])
    down = lax.broadcasted_iota(jnp.int32, (CHUNK, 3 * SUB), 0)
    sel_send[...] = jnp.where(down == send_list() % CHUNK, 1.0, 0.0).astype(bf16)
    remote[...] = jnp.zeros_like(remote)
    sendbuf[0] = jnp.zeros_like(sendbuf[0])

    outgoing(0, 8, 3)
    pl.semaphore_wait(
        barrier, 1 + has_prev.astype(jnp.int32) + has_next.astype(jnp.int32)
    )
    start(0, has_prev, has_next, True)

    for f in range(4):
        down = lax.broadcasted_iota(jnp.int32, (CHUNK, el), 0)
        sel[:, f * el : (f + 1) * el] = jnp.where(down == slot(f) % CHUNK, 1.0, 0.0).astype(bf16)

    fpad[...] = jnp.zeros_like(fpad)
    d3[...] = jnp.zeros_like(d3)
    l3[...] = jnp.zeros_like(l3)
    for b in range(3):
        hi, lo = split(deriv[b])
        d3[b * RP : b * RP + NP, :] = dot(hi, spread[0]) + dot(lo, spread[1])
    d3[3 * RP : 3 * RP + 4 * FP, :] = trace3[...].astype(f32)
    hi, lo = split(lift[...])
    l3[0:NP, :] = dot(hi, lift_spread[0]) + dot(lo, lift_spread[1])
    lane = lax.broadcasted_iota(jnp.int32, l3.shape, 1)
    lb[...] = jnp.concatenate(
        [jnp.where(lane // FP % 4 == f, l3[...], 0.0) for f in range(4)], axis=0
    ).astype(bf16)
    d3b = d3[...].astype(bf16)
    for c in range(NC):
        fpad[c, 0:NP, :] = fields[c]
        hi, lo = split(fpad[c])
        y = dot(d3b, jnp.concatenate([hi, hi, lo], axis=0))
        grads[c] = y[: 3 * RP]
        tr[c * 4 * FP : (c + 1) * 4 * FP, :] = y[3 * RP :]

    def trace_pq(f, n_ref, sign):
        at = [tr[c * 4 * FP + f * FP : c * 4 * FP + (f + 1) * FP, :] for c in range(NC)]
        sa, ca, sb, cb = (n_ref[f, i : i + 1, :] for i in range(4))
        if sign is not None:
            at[:3] = [sign * e for e in at[:3]]
        e_t = ca * (cb * at[0] + sb * at[1]) - sa * at[2]
        e_p = cb * at[1] - sb * at[0]
        h_t = ca * (cb * at[3] + sb * at[4]) - sa * at[5]
        h_p = cb * at[4] - sb * at[3]
        return jnp.concatenate([h_p - e_t, -h_t - e_p], axis=0)

    def fill_pool():
        for f in range(4):
            sign = jnp.where(nb[f : f + 1, :] < 0, -1.0, 1.0)
            pool_store(f, trace_pq(f, recv_n, sign))

    def lifted(pq):
        halves_of = []
        for at in (0, FP):
            hi, lo = split(jnp.concatenate([pq[f][at : at + FP] for f in range(4)], axis=0))
            halves_of.append(dot(lb[...], jnp.concatenate([hi, hi, lo], axis=0)))
        lp, lq = halves_of
        for c in range(NC):
            k, total = c % 3, 0.0
            a, b = (lp, lq) if c < 3 else (lq, lp)
            for f in range(4):
                at = slice(f * RP, (f + 1) * RP)
                total = total + coef[f, k : k + 1, :] * a[at]
                if k < 2:
                    term = coef[f, 3 + k : 4 + k, :] * b[at]
                    total = total + term if c < 3 else total - term
            yield c, total

    @pl.when(fine)
    def _():
        rhs6[...] = jnp.zeros_like(rhs6)
        for k in range(binv.shape[0]):
            b2 = dot(binv[k], cols6[...]).astype(bf16)
            for weights, select in ((wt, trace6), (wf, rows6)):
                half_block = dot(select[...], b2).astype(bf16)
                for at in (k * BK, k * BK + BK // 2):
                    weights[:, at : at + BK // 2] = half_block

    finish(0, has_prev, has_next, True)
    gather_all(8, recv_n)
    fill_pool()
    outgoing(1, 2 * FP, 3)
    start(1, has_prev, has_next, True)

    gather_local(2 * FP, ext)
    remote[...] = jnp.zeros_like(remote)
    finish(1, has_prev, has_next, True)
    gather_late(2 * FP, ext, 3)

    @pl.when(jnp.logical_not(fine))
    def _():
        pq = [trace_pq(f, own, None) - ext[f] for f in range(4)]

        def along(c, axis):
            return sum(
                metric[3 * axis + b : 3 * axis + b + 1, :] * grads[c, b * RP : (b + 1) * RP, :]
                for b in range(3)
            )

        for c, s in lifted(pq):
            k, other = c % 3, 3 - 3 * (c // 3)
            one, two = (k + 1) % 3, (k + 2) % 3
            curl = along(other + two, one) - along(other + one, two)
            vol = curl if c < 3 else -curl
            out[c] = (fpad[c, 0:RP, :] + STEP * (vol + s))[:NP]

    @pl.when(fine)
    def _():
        def right_side():
            terms = [
                fpad[c, 0:RP, :] - STEP * s for c, s in lifted([ext[f] for f in range(4)])
            ]
            hi, lo = split(jnp.concatenate(terms, axis=0))
            for k in range(binv.shape[0]):
                mask = jnp.where(kind[...] == k + 1, 1.0, 0.0).astype(bf16)
                for at, part in ((k * BK, hi), (k * BK + BK // 2, lo)):
                    rhs6[at : at + NC * RP, :] = part * mask

        for f in range(4):
            base[f] = jnp.where(slot(f) >= 4 * el + 2 * SUB, ext[f], 0.0)

        def sweep(no, carry):
            right_side()
            tr[...] = dot(wt[...], rhs6[...])
            fill_pool()
            outgoing(no, 2 * FP, 2)
            start(no, fine_prev, fine_next, False)
            gather_local(2 * FP, ext, base)
            finish(no, fine_prev, fine_next, False)
            gather_late(2 * FP, ext, 2)
            return carry

        lax.fori_loop(2, SWEEPS + 1, sweep, 0)
        right_side()
        total = dot(wf[...], rhs6[...])
        for c in range(NC):
            out[c] = total[c * RP : c * RP + NP]


def move_kernel(source, target, sems):
    copies = [pltpu.make_async_copy(source.at[c], target.at[c], sems.at[c]) for c in range(NC)]
    for copy in copies:
        copy.start()
    for copy in copies:
        copy.wait()


def moved(x):
    return pl.pallas_call(
        move_kernel,
        out_shape=jax.ShapeDtypeStruct(x.shape, x.dtype),
        in_specs=[pl.BlockSpec(memory_space=pl.ANY)],
        out_specs=pl.BlockSpec(memory_space=pl.ANY),
        scratch_shapes=[pltpu.SemaphoreType.DMA((NC,))],
    )(x)


def shards(*args):
    (fields, metric, scale, angles, nb, send_dom, send_part, kind, deriv, lift, binv) = args
    el = fields.shape[2]
    kinds = binv.shape[0]
    operands = [
        fields, metric, scale, angles, nb, send_dom, send_part.reshape(1, -1),
        kind.reshape(1, -1), deriv, lift, binv, *constants(),
    ]
    vmem = pltpu.VMEM
    result = pl.pallas_call(
        functools.partial(kernel, el),
        out_shape=jax.ShapeDtypeStruct(fields.shape, f32),
        in_specs=[pl.BlockSpec(memory_space=vmem)] * len(operands),
        out_specs=pl.BlockSpec(memory_space=vmem),
        scratch_shapes=[
            vmem((NC, KP, el), f32),
            vmem((3 * RP + 4 * FP, 3 * KP), f32),
            vmem((RP, 12 * FP), f32),
            vmem((NC * 4 * FP, kinds * BK), bf16),
            vmem((NC * RP, kinds * BK), bf16),
            vmem((NC, 3 * RP, el), f32),
            vmem((NC * 4 * FP, el), f32),
            vmem((4, 8, el), f32),
            vmem((4, 8, el), f32),
            vmem((4, 8, el), f32),
            vmem((CHUNK, 4 * el), bf16),
            vmem((CHUNK, 3 * SUB), bf16),
            vmem(((4 * (el // CHUNK) + 1) * 4 * FP, CHUNK), bf16),
            vmem((3, 2 * FP, SUB), f32),
            vmem((4, 2 * FP, el), f32),
            vmem((4, 2 * FP, el), f32),
            vmem((4 * RP, 12 * FP), bf16),
            vmem((kinds * BK, el), bf16),
            vmem((SWEEPS + 1, 3, 2 * FP, SUB), f32),
            vmem((SWEEPS + 1, 3, 2 * FP, SUB), f32),
            pltpu.SemaphoreType.DMA((SWEEPS + 1, 3)),
            pltpu.SemaphoreType.DMA((SWEEPS + 1, 3)),
        ],
        compiler_params=pltpu.CompilerParams(
            collective_id=0, has_side_effects=True, vmem_limit_bytes=56 * 2**20
        ),
    )(*operands)
    return moved(result)


def solution(mesh):
    both = ("group", "dom")
    in_specs = (
        P(None, None, both), P(None, both), P(None, both), P(None, None, both), P(None, both),
        P(None, both), P(both), P(both), P(), P(), P(),
    )
    return jax.shard_map(
        shards, mesh=mesh, in_specs=in_specs, out_specs=P(None, None, both), check_vma=False
    )
```

```python
import functools

import jax
import jax.numpy as jnp
import numpy as np
from jax import lax
from jax.experimental import pallas as pl
from jax.experimental.pallas import tpu as pltpu
from jax.sharding import PartitionSpec as P

SWEEPS = 4
STEP = 0.2
NC, NP, NFP = 6, 35, 15
RP = 40
KP = 48
FP = 16
CHUNK = 512
SUB = 128
f32, bf16 = jnp.float32, jnp.bfloat16


def face_nodes():
    lattice = [(r, s, t) for r in range(5) for s in range(5 - r) for t in range(5 - r - s)]
    tests = [
        lambda p: p[2] == 0,
        lambda p: p[1] == 0,
        lambda p: p[0] == 0,
        lambda p: sum(p) == 4,
    ]
    return [[i for i, p in enumerate(lattice) if test(p)] for test in tests]


def constants():
    trace = np.zeros((4 * FP, NP), np.float32)
    for f, nodes in enumerate(face_nodes()):
        for n, node in enumerate(nodes):
            trace[f * FP + n, node] = 1
    trace3 = np.zeros((4 * FP, 3 * KP), np.float32)
    trace3[:, :NP] = trace
    trace3[:, 2 * KP : 2 * KP + NP] = trace
    spread = np.zeros((2, NP, 3 * KP), np.float32)
    for i in range(NP):
        spread[0, i, i] = spread[0, i, 2 * KP + i] = spread[1, i, KP + i] = 1
    lift_spread = np.zeros((2, 4 * NFP, 3 * 4 * FP), np.float32)
    for f in range(4):
        for n in range(NFP):
            row, col = f * NFP + n, f * FP + n
            lift_spread[0, row, col] = lift_spread[0, row, 8 * FP + col] = 1
            lift_spread[1, row, 4 * FP + col] = 1
    trace6 = np.kron(np.eye(NC, dtype=np.float32), trace)
    rows6 = np.kron(np.eye(NC, dtype=np.float32), np.eye(RP, NP, dtype=np.float32))
    cols6 = np.concatenate([rows6.T, rows6.T], axis=1)
    return [jnp.asarray(a, bf16) for a in (trace3, spread, lift_spread, trace6, rows6, cols6)]


def split(x):
    hi = x.astype(bf16)
    return hi, (x - hi.astype(f32)).astype(bf16)


def dot(a, b):
    return jnp.dot(a, b, preferred_element_type=f32)


def kernel(
    el, fields, metric, scale, angles, nb, send_dom, send_part, kind, deriv, lift, binv,
    trace3, spread, lift_spread, trace6, rows6, cols6,
    out,
    fpad, d3, l3, wt, wf, grads, tr, own, recv_n, coef, sel, sel_send, pool, remote, ext, rhs,
    base, sendbuf, recvbuf, send_sem, recv_sem,
):
    grp, dom = lax.axis_index("group"), lax.axis_index("dom")
    count = lax.axis_size("dom")
    half = count // 2
    fine = jnp.logical_and(grp == 1, dom >= half)
    halves = el // CHUNK
    chunks = 4 * halves
    has_prev, has_next = dom > 0, dom < count - 1
    fine_prev = jnp.logical_and(fine, dom > half)
    fine_next = jnp.logical_and(fine, has_next)

    barrier = pltpu.get_barrier_semaphore()

    @pl.when(has_prev)
    def _():
        pl.semaphore_signal(barrier, inc=1, device_id={"dom": dom - 1})

    @pl.when(has_next)
    def _():
        pl.semaphore_signal(barrier, inc=1, device_id={"dom": dom + 1})

    pl.semaphore_signal(barrier, inc=1, device_id={"group": 1 - grp})

    def slot(f):
        row = nb[f : f + 1, :]
        lane = lax.broadcasted_iota(jnp.int32, (1, el), 1)
        return jnp.where(row < 0, lane + f * el, row)

    def send_list():
        return jnp.concatenate([send_dom[0:1, :], send_dom[1:2, :], send_part[...]], axis=1)

    def pair_copies(step):
        targets = ({"dom": dom - 1}, {"dom": dom + 1}, {"group": 1 - grp})
        lands = (1, 0, 2)
        return [
            pltpu.make_async_remote_copy(
                src_ref=sendbuf.at[step, i],
                dst_ref=recvbuf.at[step, lands[i]],
                send_sem=send_sem.at[step, i],
                recv_sem=recv_sem.at[step, lands[i]],
                device_id=targets[i],
            )
            for i in range(3)
        ]

    def start(step, to_prev, to_next, partner):
        copies = pair_copies(step)

        @pl.when(to_prev)
        def _():
            copies[0].start()

        @pl.when(to_next)
        def _():
            copies[1].start()

        if partner:
            copies[2].start()

    def finish(step, from_prev, from_next, partner):
        copies = pair_copies(step)

        @pl.when(from_prev)
        def _():
            copies[0].wait_send()
            copies[1].wait_recv()
            remote[0] = recvbuf[step, 0]

        @pl.when(from_next)
        def _():
            copies[1].wait_send()
            copies[0].wait_recv()
            remote[1] = recvbuf[step, 1]

        if partner:
            copies[2].wait()
            remote[2] = recvbuf[step, 2]

    def pool_store(f, x):
        rows = x.shape[0]
        hi = x.astype(bf16).astype(f32)
        both = jnp.concatenate([hi, x - hi], axis=0).astype(bf16)
        for k in range(halves):
            h = f * halves + k
            pool[h * 2 * rows : (h + 1) * 2 * rows, :] = both[:, k * CHUNK : (k + 1) * CHUNK]

    def pick(y, which, rows, total=None):
        if total is None:
            total = jnp.zeros((rows, y.shape[1]), f32)
        for h in range(chunks):
            at = h * 2 * rows
            value = y[at : at + rows] + y[at + rows : at + 2 * rows]
            total = jnp.where(which == h, value, total)
        return total

    def outgoing(step, rows, lists=3):
        y = dot(pool[: chunks * 2 * rows, :], sel_send[:, : lists * SUB])
        picked = pick(y, (send_list() // CHUNK)[:, : lists * SUB], rows)
        for i in range(lists):
            sendbuf[step, i, 0:rows, :] = picked[:, i * SUB : (i + 1) * SUB]

    def gather_local(rows, dest, start_from=None):
        for f in range(4):
            y = dot(pool[: chunks * 2 * rows, :], sel[:, f * el : (f + 1) * el])
            under = None if start_from is None else start_from[f]
            dest[f] = pick(y, slot(f) // CHUNK, rows, under)

    def gather_remote(rows, dest, lists=3):
        x = jnp.concatenate([remote[i, 0:rows, :] for i in range(lists)], axis=1)
        hi = x.astype(bf16).astype(f32)
        both = jnp.concatenate([hi, x - hi], axis=0).astype(bf16)
        for f in range(4):
            y = dot(both, sel[0 : lists * SUB, f * el : (f + 1) * el])
            here = slot(f)
            there = jnp.logical_and(here >= 4 * el, here < 4 * el + lists * SUB)
            dest[f] = jnp.where(there, y[:rows] + y[rows:], dest[f])

    polar, azimuth = angles[0], angles[1]
    parts = (jnp.sin(polar), jnp.cos(polar), jnp.sin(azimuth), jnp.cos(azimuth))
    own[...] = jnp.zeros_like(own)
    for f in range(4):
        for i in range(4):
            own[f, i : i + 1, :] = parts[i][f : f + 1, :]
        w = 0.5 * scale[f : f + 1, :]
        sa, ca, sb, cb = (p[f : f + 1, :] for p in parts)
        for i, row in enumerate((w * ca * cb, w * ca * sb, -w * sa, -w * sb, w * cb)):
            coef[f, i : i + 1, :] = row
        pool_store(f, own[f])
    down = lax.broadcasted_iota(jnp.int32, (CHUNK, 3 * SUB), 0)
    sel_send[...] = jnp.where(down == send_list() % CHUNK, 1.0, 0.0).astype(bf16)
    remote[...] = jnp.zeros_like(remote)
    sendbuf[0] = jnp.zeros_like(sendbuf[0])

    outgoing(0, 8)
    pl.semaphore_wait(
        barrier, 1 + has_prev.astype(jnp.int32) + has_next.astype(jnp.int32)
    )
    start(0, has_prev, has_next, True)

    for f in range(4):
        down = lax.broadcasted_iota(jnp.int32, (CHUNK, el), 0)
        sel[:, f * el : (f + 1) * el] = jnp.where(down == slot(f) % CHUNK, 1.0, 0.0).astype(bf16)
    gather_local(8, recv_n)

    fpad[...] = jnp.zeros_like(fpad)
    d3[...] = jnp.zeros_like(d3)
    l3[...] = jnp.zeros_like(l3)
    for b in range(3):
        hi, lo = split(deriv[b])
        d3[b * RP : b * RP + NP, :] = dot(hi, spread[0]) + dot(lo, spread[1])
    d3[3 * RP : 3 * RP + 4 * FP, :] = trace3[...].astype(f32)
    hi, lo = split(lift[...])
    l3[0:NP, :] = dot(hi, lift_spread[0]) + dot(lo, lift_spread[1])
    d3b = d3[...].astype(bf16)
    for c in range(NC):
        fpad[c, 0:NP, :] = fields[c]
        hi, lo = split(fpad[c])
        y = dot(d3b, jnp.concatenate([hi, hi, lo], axis=0))
        grads[c] = y[: 3 * RP]
        tr[c * 4 * FP : (c + 1) * 4 * FP, :] = y[3 * RP :]

    def trace_pq(f, n_ref, sign):
        at = [tr[c * 4 * FP + f * FP : c * 4 * FP + (f + 1) * FP, :] for c in range(NC)]
        sa, ca, sb, cb = (n_ref[f, i : i + 1, :] for i in range(4))
        if sign is not None:
            at[:3] = [sign * e for e in at[:3]]
        e_t = ca * (cb * at[0] + sb * at[1]) - sa * at[2]
        e_p = cb * at[1] - sb * at[0]
        h_t = ca * (cb * at[3] + sb * at[4]) - sa * at[5]
        h_p = cb * at[4] - sb * at[3]
        return jnp.concatenate([h_p - e_t, -h_t - e_p], axis=0)

    def fill_pool():
        for f in range(4):
            sign = jnp.where(nb[f : f + 1, :] < 0, -1.0, 1.0)
            pool_store(f, trace_pq(f, recv_n, sign))

    def lifted(pq):
        for c in range(NC):
            rows = []
            for f in range(4):
                p, q = pq[f][:FP], pq[f][FP:]
                a, b = (p, q) if c < 3 else (q, -p)
                k = c % 3
                row = coef[f, k : k + 1, :] * a
                if k < 2:
                    row = row + coef[f, 3 + k : 4 + k, :] * b
                rows.append(row)
            hi, lo = split(jnp.concatenate(rows, axis=0))
            yield c, dot(l3[...].astype(bf16), jnp.concatenate([hi, hi, lo], axis=0))

    finish(0, has_prev, has_next, True)
    gather_remote(8, recv_n)
    fill_pool()
    outgoing(1, 2 * FP)
    start(1, has_prev, has_next, True)
    gather_local(2 * FP, ext)

    @pl.when(fine)
    def _():
        for k in range(binv.shape[0]):
            b2 = dot(binv[k], cols6[...]).astype(bf16)
            wt[k] = dot(trace6[...], b2).astype(bf16)
            wf[k] = dot(rows6[...], b2).astype(bf16)

    remote[...] = jnp.zeros_like(remote)
    finish(1, has_prev, has_next, True)
    gather_remote(2 * FP, ext)

    @pl.when(jnp.logical_not(fine))
    def _():
        pq = [trace_pq(f, own, None) - ext[f] for f in range(4)]

        def along(c, axis):
            return sum(
                metric[3 * axis + b : 3 * axis + b + 1, :] * grads[c, b * RP : (b + 1) * RP, :]
                for b in range(3)
            )

        for c, s in lifted(pq):
            k, other = c % 3, 3 - 3 * (c // 3)
            one, two = (k + 1) % 3, (k + 2) % 3
            curl = along(other + two, one) - along(other + one, two)
            vol = curl if c < 3 else -curl
            out[c] = (fpad[c, 0:RP, :] + STEP * (vol + s))[:NP]

    @pl.when(fine)
    def _():
        def right_side():
            terms = [
                fpad[c, 0:RP, :] - STEP * s for c, s in lifted([ext[f] for f in range(4)])
            ]
            hi, lo = split(jnp.concatenate(terms, axis=0))
            rhs[0 : NC * RP, :] = hi
            rhs[NC * RP : 2 * NC * RP, :] = lo

        def blocks(weights, k):
            mask = jnp.where(kind[...] == k + 1, 1.0, 0.0).astype(bf16)
            return dot(weights[k], rhs[...] * mask)

        for f in range(4):
            base[f] = jnp.where(slot(f) >= 4 * el + 2 * SUB, ext[f], 0.0)

        def sweep(no, carry):
            right_side()
            tr[...] = blocks(wt, 0)
            for k in range(1, binv.shape[0]):
                tr[...] += blocks(wt, k)
            fill_pool()
            outgoing(no, 2 * FP, 2)
            start(no, fine_prev, fine_next, False)
            gather_local(2 * FP, ext, base)
            finish(no, fine_prev, fine_next, False)
            gather_remote(2 * FP, ext, 2)
            return carry

        lax.fori_loop(2, SWEEPS + 1, sweep, 0)
        right_side()
        total = blocks(wf, 0)
        for k in range(1, binv.shape[0]):
            total += blocks(wf, k)
        for c in range(NC):
            out[c] = total[c * RP : c * RP + NP]


def shards(*args):
    (fields, metric, scale, angles, nb, send_dom, send_part, kind, deriv, lift, binv) = args
    el = fields.shape[2]
    kinds = binv.shape[0]
    operands = [
        fields, metric, scale, angles, nb, send_dom, send_part.reshape(1, -1),
        kind.reshape(1, -1), deriv, lift, binv, *constants(),
    ]
    vmem = pltpu.VMEM
    return pl.pallas_call(
        functools.partial(kernel, el),
        out_shape=jax.ShapeDtypeStruct(fields.shape, f32),
        in_specs=[pl.BlockSpec(memory_space=vmem)] * len(operands),
        out_specs=pl.BlockSpec(memory_space=vmem),
        scratch_shapes=[
            vmem((NC, KP, el), f32),
            vmem((3 * RP + 4 * FP, 3 * KP), f32),
            vmem((RP, 12 * FP), f32),
            vmem((kinds, NC * 4 * FP, 2 * NC * RP), bf16),
            vmem((kinds, NC * RP, 2 * NC * RP), bf16),
            vmem((NC, 3 * RP, el), f32),
            vmem((NC * 4 * FP, el), f32),
            vmem((4, 8, el), f32),
            vmem((4, 8, el), f32),
            vmem((4, 8, el), f32),
            vmem((CHUNK, 4 * el), bf16),
            vmem((CHUNK, 3 * SUB), bf16),
            vmem((4 * (el // CHUNK) * 4 * FP, CHUNK), bf16),
            vmem((3, 2 * FP, SUB), f32),
            vmem((4, 2 * FP, el), f32),
            vmem((2 * NC * RP, el), bf16),
            vmem((4, 2 * FP, el), f32),
            vmem((SWEEPS + 1, 3, 2 * FP, SUB), f32),
            vmem((SWEEPS + 1, 3, 2 * FP, SUB), f32),
            pltpu.SemaphoreType.DMA((SWEEPS + 1, 3)),
            pltpu.SemaphoreType.DMA((SWEEPS + 1, 3)),
        ],
        compiler_params=pltpu.CompilerParams(
            collective_id=0, has_side_effects=True, vmem_limit_bytes=56 * 2**20
        ),
    )(*operands)


def solution(mesh):
    both = ("group", "dom")
    in_specs = (
        P(None, None, both), P(None, both), P(None, both), P(None, None, both), P(None, both),
        P(None, both), P(both), P(both), P(), P(), P(),
    )
    return jax.shard_map(
        shards, mesh=mesh, in_specs=in_specs, out_specs=P(None, None, both), check_vma=False
    )
```
